32 devices in a mesh: ctx: 16 (over z, y, x), tp: 2 (over core).
Axes of the slice: x: 2, y: 2, z: 4, core: 2. Of those that a mesh axis runs over, the one named last changes fastest.
Arguments:
- queries: bfloat16 [12288, 8192], P('ctx', 'tp'), may hold values from -6 to 6
- keys: bfloat16 [12288, 8192], P('ctx', 'tp'), may hold values from -6 to 6
- values: bfloat16 [12288, 8192], P('ctx', 'tp'), may hold values from -40 to 40
- out_grad: bfloat16 [12288, 8192], P('ctx', 'tp'), may hold values from -6 to 6
- gain: float32 [8192], P('tp'), may hold values from 0.1 to 1.9
- doc_ids: int32 [12288], P('ctx'), may hold values from 0 to 3, never falling along the last dimension, each value on 1 to 6144 neighbouring positions
Outputs:
- normed: bfloat16 [12288, 8192], P('ctx', 'tp')
- grad_query: bfloat16 [12288, 8192], P('ctx', 'tp')
- grad_key: bfloat16 [12288, 8192], P('ctx', 'tp')
- grad_value: bfloat16 [12288, 8192], P('ctx', 'tp')
The draws below stay inside these ranges and needn't reach their ends.
Inputs may be any that keep to these rules, and one draw needn't show every extreme that they name: doc_ids never fall along the sequence; every one of the 4 documents has 1 to 6144 tokens and one has exactly 6144.
All inputs are finite; a program needn't handle non-finite values.
Results may differ from the reference program's by a relative error of at most 0.0062.
Values may be sent and summed in bfloat16 or wider, within the bound.
A program may use at most 256 MiB of HBM per device.

```python
import math
import jax
import jax.numpy as jnp
import numpy as np
from jax import lax

HEADS = 64
HD = 128
TOK_DEV = 768
TOKENS = 12288
DOCS = 4
DOC_MOST = 6144
N_CTX = 16


def draw_values(key, part):
    key_base, key_column, key_row = jax.random.split(key, 3)
    column = jnp.arange(HEADS * HD)
    head_rise = 3.0 ** ((column // HD).astype(jnp.float32) / (HEADS - 1))
    column_scale = jnp.exp(jax.random.uniform(key_column, (HEADS * HD,), jnp.float32, 0.0, 2.302585))
    row_scale = jnp.exp(jax.random.uniform(key_row, (TOKENS, 1), jnp.float32, 0.0, 2.302585))
    base = jnp.clip(jax.random.normal(key_base, (TOKENS, HEADS * HD), jnp.float32), -4.0, 4.0)
    return (base * head_rise[None, :] * column_scale[None, :] * row_scale / 30.0).astype(jnp.bfloat16)


def level_of(rng, dims, cuts, least, high):
    loudness = 1.0
    for dim, shards_of in cuts:
        heights = jax.random.uniform(jax.random.fold_in(jax.random.fold_in(rng, 6), dim), (shards_of,), jnp.float32, least / len(cuts), high / len(cuts))
        loudness = loudness * jnp.repeat(jnp.exp(heights), dims[dim] // shards_of).reshape((-1,) + (1,) * (len(dims) - 1 - dim))
    return loudness


def profile(number_of, total, limit, lean):
    weights = [(1 << 20) // math.isqrt(standing ** lean) + 1 for standing in range(2, number_of + 1)]
    rest, counts = total - limit - (number_of - 1), [1] * (number_of - 1)
    while rest > 0:
        candidates = [i for i in range(number_of - 1) if counts[i] < limit]
        pool, budget = sum([weights[i] for i in candidates]), rest
        for i in candidates:
            more = min(limit - counts[i], max(1, budget * weights[i] // pool), rest)
            counts[i] = counts[i] + more
            rest = rest - more
    return np.array([limit] + counts)


def ragged(key, number_of, total, bound, skew):
    if number_of == 2:
        one = jax.random.randint(key, (), max(1, total - bound), min(bound, total - 1) + 1)
        return jnp.stack([one, total - one])
    tallies = jnp.asarray(profile(number_of, total, bound, skew), jnp.int32)
    pairs = (number_of - 1) // 2
    giver, receiver = tallies[1:1 + 2 * pairs:2], tallies[2:2 + 2 * pairs:2]
    slack = jnp.minimum(giver - 1, bound - receiver)
    passed = jax.random.randint(jax.random.fold_in(key, 1), (pairs,), 0, 1 << 20) % (slack + 1)
    tallies = tallies.at[1:1 + 2 * pairs:2].set(giver - passed).at[2:2 + 2 * pairs:2].set(receiver + passed)
    return tallies[jax.random.permutation(jax.random.fold_in(key, 2), number_of)]


def centred(stream_key, shape, spread, bound, cuts=(), kind=jnp.bfloat16):
    entries = jax.random.normal(stream_key, shape, jnp.float32) * spread
    if len(cuts) > 0:
        entries = level_of(stream_key, shape, cuts, -0.22, 0.18) * entries
    return jnp.clip(entries, min=-bound, max=bound).astype(kind)


def setup_inputs(seed: int = 0) -> dict:
    key_of = jax.random.split(jax.random.key(seed), 7)
    queries = centred(key_of[0], (TOKENS, HEADS * HD), 1.0, 6.0, ((0, 16), (1, 2)))
    keys = centred(key_of[1], (TOKENS, HEADS * HD), 1.0, 6.0, ((0, 16), (1, 2)))
    values = draw_values(jax.random.fold_in(key_of[6], 71), 0)
    out_grad = centred(key_of[3], (TOKENS, HEADS * HD), 1.0, 6.0, ((0, 16), (1, 2)))
    gain = jnp.clip(1.0 + 0.18 * jax.random.normal(key_of[4], (HEADS * HD,), jnp.float32), 0.1, 1.9)
    doc_ids = jnp.searchsorted(jnp.cumsum(ragged(key_of[5], DOCS, TOKENS, DOC_MOST, 1)), jnp.arange(TOKENS), side="right").astype(jnp.int32)
    return dict(queries=queries, keys=keys, values=values, out_grad=out_grad, gain=gain, doc_ids=doc_ids)


NORM_EPS = 1e-06

def product(form, left, right):
    return jnp.einsum(form, left.astype(jnp.float32), right.astype(jnp.float32))

def doc_mask_of(doc_block):
    position = jnp.arange(TOK_DEV)
    same_doc = doc_block[:, None] == doc_block[None, :]
    return (same_doc & (position[:, None] >= position[None, :])).astype(jnp.float32)

def reference(queries, keys, values, out_grad, gain, doc_ids):
    width = HEADS * HD
    query_blocks = queries.reshape(N_CTX, TOK_DEV, HEADS, HD)
    key_blocks = keys.reshape(N_CTX, TOK_DEV, HEADS, HD)
    value_blocks = values.reshape(N_CTX, TOK_DEV, HEADS, HD)
    grad_blocks = out_grad.reshape(N_CTX, TOK_DEV, width)
    doc_blocks = doc_ids.reshape(N_CTX, TOK_DEV)
    first_docs = doc_blocks[:, 0]
    last_docs = doc_blocks[:, TOK_DEV - 1]

    def forward_state(pieces):
        key_block, value_block, doc_block = pieces
        chosen = (doc_block == doc_block[TOK_DEV - 1]).astype(jnp.float32)
        return product('tha,thb->hab', key_block * chosen[:, None, None], value_block).astype(jnp.bfloat16)
    states = lax.map(forward_state, (key_blocks, value_blocks, doc_blocks))
    start_state = (jnp.zeros((HEADS, HD, HD), jnp.float32), jnp.int32(-1))

    def carry_forward(carried, pieces):
        running, running_doc = carried
        block_state, first_doc, last_doc = pieces
        arriving = jnp.where(running_doc == first_doc, running, 0.0).astype(jnp.bfloat16)
        running = jnp.where(running_doc == last_doc, running, 0.0) + block_state.astype(jnp.float32)
        return ((running, last_doc), arriving)
    _, incoming = lax.scan(carry_forward, start_state, (states, first_docs, last_docs))

    def middle(pieces):
        query_block, key_block, value_block, grad_block, doc_block, arriving = pieces
        doc_mask = doc_mask_of(doc_block)
        first_rows = (doc_block == doc_block[0]).astype(jnp.float32)[:, None, None]
        scores = (product('tha,sha->hts', query_block, key_block) * doc_mask[None]).astype(jnp.bfloat16)
        attended = product('hts,shb->thb', scores, value_block) + product('tha,hab->thb', query_block, arriving) * first_rows
        flat = attended.reshape(TOK_DEV, width)
        inverse = lax.rsqrt(lax.optimization_barrier(jnp.sum(flat * flat, axis=1)) / width + NORM_EPS)
        normed = (flat * inverse[:, None] * gain[None, :]).astype(jnp.bfloat16)
        scaled_grad = gain[None, :] * grad_block.astype(jnp.float32)
        cross_sum = lax.optimization_barrier(jnp.sum(scaled_grad * flat, axis=1))
        delta = (inverse[:, None] * scaled_grad - flat * (inverse ** 3 * cross_sum / width)[:, None]).astype(jnp.bfloat16)
        delta_rows = delta.reshape(TOK_DEV, HEADS, HD)
        reverse_state = product('tha,thb->hab', query_block * first_rows, delta_rows).astype(jnp.bfloat16)
        dscores = (product('thb,shb->hts', delta_rows, value_block) * doc_mask[None]).astype(jnp.bfloat16)
        grad_query = product('hts,sha->tha', dscores, key_block) + product('thb,hab->tha', delta_rows, arriving) * first_rows
        return (normed, grad_query.astype(jnp.bfloat16), delta_rows, reverse_state)
    normed, grad_query, deltas, reverse_states = lax.map(middle, (query_blocks, key_blocks, value_blocks, grad_blocks, doc_blocks, incoming))

    def carry_backward(carried, pieces):
        running, running_doc = carried
        block_state, first_doc, last_doc = pieces
        leaving = jnp.where(running_doc == last_doc, running, 0.0).astype(jnp.bfloat16)
        running = jnp.where(running_doc == first_doc, running, 0.0) + block_state.astype(jnp.float32)
        return ((running, first_doc), leaving)
    _, outgoing = lax.scan(carry_backward, start_state, (reverse_states, first_docs, last_docs), reverse=True)

    def finish(pieces):
        query_block, key_block, value_block, delta_rows, doc_block, leaving = pieces
        doc_mask = doc_mask_of(doc_block)
        last_rows = (doc_block == doc_block[TOK_DEV - 1]).astype(jnp.float32)[:, None, None]
        scores = (product('tha,sha->hts', query_block, key_block) * doc_mask[None]).astype(jnp.bfloat16)
        dscores = (product('thb,shb->hts', delta_rows, value_block) * doc_mask[None]).astype(jnp.bfloat16)
        grad_key = product('hts,tha->sha', dscores, query_block) + product('thb,hab->tha', value_block, leaving) * last_rows
        grad_value = product('hts,thb->shb', scores, delta_rows) + product('tha,hab->thb', key_block, leaving) * last_rows
        return (grad_key.astype(jnp.bfloat16), grad_value.astype(jnp.bfloat16))
    grad_key, grad_value = lax.map(finish, (query_blocks, key_blocks, value_blocks, deltas, doc_blocks, outgoing))
    return (normed.reshape(TOKENS, width), grad_query.reshape(TOKENS, width), grad_key.reshape(TOKENS, width), grad_value.reshape(TOKENS, width))
```

```python
import functools

import jax
import jax.numpy as jnp
from jax import lax
from jax.experimental import pallas as pl
from jax.experimental.pallas import tpu as pltpu
from jax.sharding import PartitionSpec as P

HEADS = 64
HD = 128
NORM_EPS = 1e-06
MEMBERS = 4
CHUNKS = 2
ROWS = 256
F32 = jnp.float32
BF16 = jnp.bfloat16


def dot_nn(a, b):
    return lax.dot_general(a, b, (((1,), (0,)), ((), ())), preferred_element_type=F32)


def dot_nt(a, b):
    return lax.dot_general(a, b, (((1,), (1,)), ((), ())), preferred_element_type=F32)


def dot_tn(a, b):
    return lax.dot_general(a, b, (((0,), (0,)), ((), ())), preferred_element_type=F32)


def state_kernel(k_ref, v_ref, last_ref, state_ref):
    for h in range(k_ref.shape[1] // HD):
        cols = slice(h * HD, (h + 1) * HD)
        state_ref[cols, :] = dot_tn(k_ref[:, cols] * last_ref[...], v_ref[:, cols]).astype(BF16)


def exchange_kernel(groups, reverse, state_ref, tag_ref, out_ref, got, tags, chain_in, chain_out,
                    chain_tag, sends, back, sem_a, sem_b, sem_c, sem_d, sem_e):
    me = lax.axis_index("ctx")
    group, member = me // MEMBERS, me % MEMBERS
    step = -1 if reverse else 1
    place = groups - 1 - group if reverse else group
    have, need = (0, 1) if reverse else (1, 0)
    tail = 0 if reverse else MEMBERS - 1
    part = state_ref.shape[0] // MEMBERS
    piece = part // CHUNKS
    ahead = (group + step + groups) % groups * MEMBERS + member
    behind = (group - step + groups) % groups * MEMBERS + member

    barrier = pltpu.get_barrier_semaphore()
    for r in range(1, MEMBERS):
        pl.semaphore_signal(barrier, inc=1, device_id={"ctx": group * MEMBERS + (member + r) % MEMBERS})
    pl.semaphore_signal(barrier, inc=1, device_id={"ctx": ahead})
    pl.semaphore_signal(barrier, inc=1, device_id={"ctx": behind})
    pl.semaphore_wait(barrier, MEMBERS + 1)

    def scatter(m, slot):
        return pltpu.make_async_remote_copy(
            src_ref=state_ref.at[pl.ds(m * part, part)], dst_ref=got.at[slot],
            send_sem=sem_a.at[0, m], recv_sem=sem_a.at[1, slot], device_id={"ctx": group * MEMBERS + m})

    def label(m, slot):
        return pltpu.make_async_remote_copy(
            src_ref=tag_ref, dst_ref=tags.at[slot],
            send_sem=sem_b.at[0, m], recv_sem=sem_b.at[1, slot], device_id={"ctx": group * MEMBERS + m})

    def chain(c):
        return pltpu.make_async_remote_copy(
            src_ref=chain_out.at[c], dst_ref=chain_in.at[c],
            send_sem=sem_c.at[0, c], recv_sem=sem_c.at[1, c], device_id={"ctx": ahead})

    def chain_label():
        return pltpu.make_async_remote_copy(
            src_ref=tags.at[tail], dst_ref=chain_tag,
            send_sem=sem_d.at[0], recv_sem=sem_d.at[1], device_id={"ctx": ahead})

    def give(m, slot, c):
        return pltpu.make_async_remote_copy(
            src_ref=sends.at[m, c], dst_ref=back.at[slot, c],
            send_sem=sem_e.at[0, m, c], recv_sem=sem_e.at[1, slot, c], device_id={"ctx": group * MEMBERS + m})

    for m in range(MEMBERS):
        @pl.when(m != member)
        def _(m=m):
            label(m, member).start()
            scatter(m, member).start()

        @pl.when(m == member)
        def _(m=m):
            tags[m] = tag_ref[...]
            got[m] = state_ref[m * part:(m + 1) * part, :]

    @pl.when(place == 0)
    def _():
        chain_tag[...] = jnp.full_like(chain_tag, -1.0)
        chain_in[...] = jnp.zeros_like(chain_in)

    for m in range(MEMBERS):
        @pl.when(m != member)
        def _(m=m):
            label(m, m).wait_recv()

    @pl.when(place < groups - 1)
    def _():
        chain_label().start()

    for m in range(MEMBERS):
        @pl.when(m != member)
        def _(m=m):
            scatter(m, m).wait_recv()

    @pl.when(place > 0)
    def _():
        chain_label().wait_recv()

    def equal(a, b):
        return (a == b).astype(F32)

    haves = [tags[m, have:have + 1, :] for m in range(MEMBERS)]
    needs = [tags[m, need:need + 1, :] for m in range(MEMBERS)]
    before = chain_tag[have:have + 1, :]
    order = range(MEMBERS - 1, -1, -1) if reverse else range(MEMBERS)
    for c in range(CHUNKS):
        rows = slice(c * piece, (c + 1) * piece)
        total = jnp.zeros((piece, HD), F32)
        for m in range(MEMBERS):
            total += equal(haves[m], haves[tail]) * got[m, rows, :].astype(F32)

        @pl.when(place > 0)
        def _(c=c):
            chain(c).wait_recv()

        arrived = chain_in[c].astype(F32)
        chain_out[c] = (total + equal(before, haves[tail]) * arrived).astype(BF16)

        @pl.when(place < groups - 1)
        def _(c=c):
            chain(c).start()

        done = []
        for m in order:
            own = equal(before, needs[m]) * arrived
            for j in done:
                own += equal(haves[j], needs[m]) * got[j, rows, :].astype(F32)
            done.append(m)
            own = own.astype(BF16)

            @pl.when(m != member)
            def _(m=m, c=c, own=own):
                sends[m, c] = own
                give(m, member, c).start()

            @pl.when(m == member)
            def _(m=m, c=c, own=own):
                back[m, c] = own

    for m in range(MEMBERS):
        for c in range(CHUNKS):
            @pl.when(m != member)
            def _(m=m, c=c):
                give(m, m, c).wait_recv()
            out_ref[m * part + c * piece:m * part + (c + 1) * piece, :] = back[m, c]

    for m in range(MEMBERS):
        @pl.when(m != member)
        def _(m=m):
            label(m, member).wait_send()
            scatter(m, member).wait_send()
            for c in range(CHUNKS):
                give(m, member, c).wait_send()

    @pl.when(place < groups - 1)
    def _():
        chain_label().wait_send()
        for c in range(CHUNKS):
            chain(c).wait_send()


def exchange(state, tag, blocks, reverse):
    groups = blocks // MEMBERS
    part = state.shape[0] // MEMBERS
    piece = part // CHUNKS
    vmem = pl.BlockSpec(memory_space=pltpu.VMEM)
    return pl.pallas_call(
        functools.partial(exchange_kernel, groups, reverse),
        out_shape=jax.ShapeDtypeStruct(state.shape, BF16),
        in_specs=[vmem, vmem],
        out_specs=vmem,
        scratch_shapes=[
            pltpu.VMEM((MEMBERS, part, HD), BF16),
            pltpu.VMEM((MEMBERS, 8, HD), F32),
            pltpu.VMEM((CHUNKS, piece, HD), BF16),
            pltpu.VMEM((CHUNKS, piece, HD), BF16),
            pltpu.VMEM((8, HD), F32),
            pltpu.VMEM((MEMBERS, CHUNKS, piece, HD), BF16),
            pltpu.VMEM((MEMBERS, CHUNKS, piece, HD), BF16),
            pltpu.SemaphoreType.DMA((2, MEMBERS)),
            pltpu.SemaphoreType.DMA((2, MEMBERS)),
            pltpu.SemaphoreType.DMA((2, CHUNKS)),
            pltpu.SemaphoreType.DMA((2,)),
            pltpu.SemaphoreType.DMA((2, MEMBERS, CHUNKS)),
        ],
        compiler_params=pltpu.CompilerParams(collective_id=1 if reverse else 0, has_side_effects=True,
                                             vmem_limit_bytes=16 * 2**20),
        name="exchange_back" if reverse else "exchange_on",
    )(state, tag)


def forward_kernel(q_ref, k_ref, v_ref, og_ref, gain_ref, inc_ref, mask_ref, first_ref,
                   att_ref, square_ref, cross_ref):
    @pl.when(pl.program_id(0) == 0)
    def _():
        square_ref[...] = jnp.zeros_like(square_ref)
        cross_ref[...] = jnp.zeros_like(cross_ref)

    tokens = q_ref.shape[0]
    for h in range(q_ref.shape[1] // HD):
        cols = slice(h * HD, (h + 1) * HD)
        for start in range(0, tokens, ROWS):
            stop = start + ROWS
            rows = slice(start, stop)
            q = q_ref[rows, cols]
            scores = dot_nt(q, k_ref[:stop, cols]).astype(BF16) * mask_ref[rows, :stop]
            att = dot_nn(scores, v_ref[:stop, cols])
            att += dot_nn(q * first_ref[rows, :], inc_ref[cols, :])
            att_ref[rows, cols] = att
            square_ref[rows, :] += att * att
            cross_ref[rows, :] += gain_ref[:, cols] * og_ref[rows, cols].astype(F32) * att


def delta_kernel(att_ref, og_ref, q_ref, gain_ref, inverse_ref, weight_ref, first_ref,
                 normed_ref, delta_ref, state_ref):
    for h in range(q_ref.shape[1] // HD):
        cols = slice(h * HD, (h + 1) * HD)
        att = att_ref[:, cols]
        gain = gain_ref[:, cols]
        inverse = inverse_ref[...]
        normed_ref[:, cols] = (att * inverse * gain).astype(BF16)
        delta = (inverse * (gain * og_ref[:, cols].astype(F32)) - att * weight_ref[...]).astype(BF16)
        delta_ref[:, cols] = delta
        state_ref[cols, :] = dot_tn(q_ref[:, cols] * first_ref[...], delta).astype(BF16)


def backward_kernel(q_ref, k_ref, v_ref, d_ref, inc_ref, out_ref, mask_ref, first_ref, last_ref,
                    gq_ref, gk_ref, gv_ref):
    tokens = q_ref.shape[0]
    for h in range(q_ref.shape[1] // HD):
        cols = slice(h * HD, (h + 1) * HD)
        grad_query = dot_nt(d_ref[:, cols] * first_ref[...], inc_ref[cols, :])
        pieces = [grad_query[r:r + ROWS] for r in range(0, tokens, ROWS)]
        for start in range(0, tokens, ROWS):
            rows = slice(start, start + ROWS)
            k, v = k_ref[rows, cols], v_ref[rows, cols]
            q, d = q_ref[start:, cols], d_ref[start:, cols]
            mask = mask_ref[rows, start:]
            last = last_ref[rows, :]
            scores = dot_nt(k, q).astype(BF16) * mask
            dscores = dot_nt(v, d).astype(BF16) * mask
            gv_ref[rows, cols] = (dot_nn(scores, d) + dot_nn(k * last, out_ref[cols, :])).astype(BF16)
            gk_ref[rows, cols] = (dot_nn(dscores, q) + dot_nt(v * last, out_ref[cols, :])).astype(BF16)
            more = dot_tn(dscores, k)
            for i in range(start // ROWS, tokens // ROWS):
                at = i * ROWS - start
                pieces[i] = pieces[i] + more[at:at + ROWS]
        for i, piece in enumerate(pieces):
            gq_ref[i * ROWS:(i + 1) * ROWS, cols] = piece.astype(BF16)


def shards(blocks, queries, keys, values, out_grad, gain, doc_ids):
    tokens, width = queries.shape
    heads = width // HD
    width_all = HEADS * HD
    position = jnp.arange(tokens)
    same = doc_ids[:, None] == doc_ids[None, :]
    mask = (same & (position[:, None] >= position[None, :])).astype(BF16)
    mask_t = (same & (position[:, None] <= position[None, :])).astype(BF16)
    first_doc, last_doc = doc_ids[0], doc_ids[tokens - 1]
    first_rows = jnp.broadcast_to((doc_ids == first_doc).astype(BF16)[:, None], (tokens, HD))
    last_rows = jnp.broadcast_to((doc_ids == last_doc).astype(BF16)[:, None], (tokens, HD))
    tag = jnp.where(jnp.arange(8)[:, None] == 0, first_doc, last_doc).astype(F32)
    tag = jnp.broadcast_to(tag, (8, HD))
    gain = gain[None, :]

    each = 2
    wide = each * HD
    grid = (heads // each,)
    head_cols = pl.BlockSpec((tokens, wide), lambda i: (0, i))
    gain_cols = pl.BlockSpec((1, wide), lambda i: (0, i))
    head_state = pl.BlockSpec((wide, HD), lambda i: (i, 0))
    whole = pl.BlockSpec((tokens, HD), lambda i: (0, 0))
    whole_mask = pl.BlockSpec((tokens, tokens), lambda i: (0, 0))
    state_shape = jax.ShapeDtypeStruct((width, HD), BF16)
    flat_shape = jax.ShapeDtypeStruct((tokens, width), BF16)
    sums_shape = jax.ShapeDtypeStruct((tokens, HD), F32)
    params = pltpu.CompilerParams(vmem_limit_bytes=40 * 2**20)

    own_state = pl.pallas_call(
        state_kernel, grid=grid, in_specs=[head_cols, head_cols, whole], out_specs=head_state,
        out_shape=state_shape, compiler_params=params, name="block_state",
    )(keys, values, last_rows)
    incoming = exchange(own_state, tag, blocks, False)
    attended, squares, crosses = pl.pallas_call(
        forward_kernel, grid=grid,
        in_specs=[head_cols, head_cols, head_cols, head_cols, gain_cols, head_state, whole_mask, whole],
        out_specs=[head_cols, whole, whole],
        out_shape=[jax.ShapeDtypeStruct((tokens, width), F32), sums_shape, sums_shape],
        compiler_params=params, name="attend",
    )(queries, keys, values, out_grad, gain, incoming, mask, first_rows)
    square_sum, cross_sum = lax.psum((jnp.sum(squares, axis=1), jnp.sum(crosses, axis=1)), "tp")
    inverse = lax.rsqrt(square_sum / width_all + NORM_EPS)
    weight = inverse**3 * cross_sum / width_all
    inverse = jnp.broadcast_to(inverse[:, None], (tokens, HD))
    weight = jnp.broadcast_to(weight[:, None], (tokens, HD))
    normed, delta, own_reverse = pl.pallas_call(
        delta_kernel, grid=grid,
        in_specs=[head_cols, head_cols, head_cols, gain_cols, whole, whole, whole],
        out_specs=[head_cols, head_cols, head_state],
        out_shape=[flat_shape, flat_shape, state_shape],
        compiler_params=params, name="delta",
    )(attended, out_grad, queries, gain, inverse, weight, first_rows)
    outgoing = exchange(own_reverse, tag, blocks, True)
    grad_query, grad_key, grad_value = pl.pallas_call(
        backward_kernel, grid=grid,
        in_specs=[head_cols] * 4 + [head_state] * 2 + [whole_mask, whole, whole],
        out_specs=[head_cols] * 3, out_shape=[flat_shape] * 3,
        compiler_params=params, name="grads",
    )(queries, keys, values, delta, incoming, outgoing, mask_t, first_rows, last_rows)
    return normed, grad_query, grad_key, grad_value


def solution(mesh):
    in_specs = (P("ctx", "tp"), P("ctx", "tp"), P("ctx", "tp"), P("ctx", "tp"), P("tp"), P("ctx"))
    out_specs = (P("ctx", "tp"), P("ctx", "tp"), P("ctx", "tp"), P("ctx", "tp"))
    return jax.shard_map(functools.partial(shards, mesh.shape["ctx"]), mesh=mesh, in_specs=in_specs,
                         out_specs=out_specs, check_vma=False)
```

```python
import functools

import jax
import jax.numpy as jnp
from jax import lax
from jax.experimental import pallas as pl
from jax.experimental.pallas import tpu as pltpu
from jax.sharding import PartitionSpec as P

HEADS = 64
HD = 128
NORM_EPS = 1e-06
MEMBERS = 4
CHUNKS = 2
ROWS = 256
F32 = jnp.float32
BF16 = jnp.bfloat16


def dot_nn(a, b):
    return lax.dot_general(a, b, (((1,), (0,)), ((), ())), preferred_element_type=F32)


def dot_nt(a, b):
    return lax.dot_general(a, b, (((1,), (1,)), ((), ())), preferred_element_type=F32)


def dot_tn(a, b):
    return lax.dot_general(a, b, (((0,), (0,)), ((), ())), preferred_element_type=F32)


def exchange(groups, reverse, make_part, work, early, spread, pairs, state_ref, tag_ref, out_ref, got, tags,
             chain_in, chain_out, chain_tag, sends, back, sem_a, sem_b, sem_c, sem_d, sem_e):
    me = lax.axis_index("ctx")
    group, member = me // MEMBERS, me % MEMBERS
    step = -1 if reverse else 1
    place = groups - 1 - group if reverse else group
    have, need = (0, 1) if reverse else (1, 0)
    tail = 0 if reverse else MEMBERS - 1
    part = state_ref.shape[0] // MEMBERS
    piece = part // CHUNKS
    ahead = (group + step + groups) % groups * MEMBERS + member
    behind = (group - step + groups) % groups * MEMBERS + member

    barrier = pltpu.get_barrier_semaphore()
    for r in range(1, MEMBERS):
        pl.semaphore_signal(barrier, inc=1, device_id={"ctx": group * MEMBERS + (member + r) % MEMBERS})
    pl.semaphore_signal(barrier, inc=1, device_id={"ctx": ahead})
    pl.semaphore_signal(barrier, inc=1, device_id={"ctx": behind})
    pl.semaphore_wait(barrier, MEMBERS + 1)

    def scatter(m, slot):
        return pltpu.make_async_remote_copy(
            src_ref=state_ref.at[pl.ds(m * part, part)], dst_ref=got.at[slot],
            send_sem=sem_a.at[0, m], recv_sem=sem_a.at[1, slot], device_id={"ctx": group * MEMBERS + m})

    def label(m, slot):
        return pltpu.make_async_remote_copy(
            src_ref=tag_ref, dst_ref=tags.at[slot],
            send_sem=sem_b.at[0, m], recv_sem=sem_b.at[1, slot], device_id={"ctx": group * MEMBERS + m})

    def chain(c):
        return pltpu.make_async_remote_copy(
            src_ref=chain_out.at[c], dst_ref=chain_in.at[c],
            send_sem=sem_c.at[0, c], recv_sem=sem_c.at[1, c], device_id={"ctx": ahead})

    def chain_label():
        return pltpu.make_async_remote_copy(
            src_ref=tags.at[tail], dst_ref=chain_tag,
            send_sem=sem_d.at[0], recv_sem=sem_d.at[1], device_id={"ctx": ahead})

    def give(m, slot, c):
        return pltpu.make_async_remote_copy(
            src_ref=sends.at[m, c], dst_ref=back.at[slot, c],
            send_sem=sem_e.at[0, m, c], recv_sem=sem_e.at[1, slot, c], device_id={"ctx": group * MEMBERS + m})

    for m in range(MEMBERS):
        @pl.when(m != member)
        def _(m=m):
            label(m, member).start()

        @pl.when(m == member)
        def _(m=m):
            tags[m] = tag_ref[...]

    for m in range(MEMBERS):
        make_part(m)

        @pl.when(m != member)
        def _(m=m):
            scatter(m, member).start()

        @pl.when(m == member)
        def _(m=m):
            got[m] = state_ref[m * part:(m + 1) * part, :]

    @pl.when(place == 0)
    def _():
        chain_tag[...] = jnp.full_like(chain_tag, -1.0)
        chain_in[...] = jnp.zeros_like(chain_in)

    for m in range(MEMBERS):
        @pl.when(m != member)
        def _(m=m):
            label(m, m).wait_recv()

    @pl.when(place < groups - 1)
    def _():
        chain_label().start()

    work(0, early)
    for m in range(MEMBERS):
        @pl.when(m != member)
        def _(m=m):
            scatter(m, m).wait_recv()

    middle = jnp.minimum(early + place * spread, pairs)
    work(early, middle)

    @pl.when(place > 0)
    def _():
        chain_label().wait_recv()

    def equal(a, b):
        return (a == b).astype(F32)

    haves = [tags[m, have:have + 1, :] for m in range(MEMBERS)]
    needs = [tags[m, need:need + 1, :] for m in range(MEMBERS)]
    before = chain_tag[have:have + 1, :]
    order = range(MEMBERS - 1, -1, -1) if reverse else range(MEMBERS)
    for c in range(CHUNKS):
        rows = slice(c * piece, (c + 1) * piece)
        total = jnp.zeros((piece, HD), F32)
        for m in range(MEMBERS):
            total += equal(haves[m], haves[tail]) * got[m, rows, :].astype(F32)

        @pl.when(place > 0)
        def _(c=c):
            chain(c).wait_recv()

        arrived = chain_in[c].astype(F32)
        chain_out[c] = (total + equal(before, haves[tail]) * arrived).astype(BF16)

        @pl.when(place < groups - 1)
        def _(c=c):
            chain(c).start()

        done = []
        for m in order:
            own = equal(before, needs[m]) * arrived
            for j in done:
                own += equal(haves[j], needs[m]) * got[j, rows, :].astype(F32)
            done.append(m)
            own = own.astype(BF16)

            @pl.when(m != member)
            def _(m=m, c=c, own=own):
                sends[m, c] = own
                give(m, member, c).start()

            @pl.when(m == member)
            def _(m=m, c=c, own=own):
                back[m, c] = own

    work(middle, pairs)
    for m in range(MEMBERS):
        for c in range(CHUNKS):
            @pl.when(m != member)
            def _(m=m, c=c):
                give(m, m, c).wait_recv()
            out_ref[m * part + c * piece:m * part + (c + 1) * piece, :] = back[m, c]

    for m in range(MEMBERS):
        @pl.when(m != member)
        def _(m=m):
            label(m, member).wait_send()
            scatter(m, member).wait_send()
            for c in range(CHUNKS):
                give(m, member, c).wait_send()

    @pl.when(place < groups - 1)
    def _():
        chain_label().wait_send()
        for c in range(CHUNKS):
            chain(c).wait_send()


def exchange_scratch(width):
    part = width // MEMBERS
    piece = part // CHUNKS
    return [
        pltpu.VMEM((MEMBERS, part, HD), BF16),
        pltpu.VMEM((MEMBERS, 8, HD), F32),
        pltpu.VMEM((CHUNKS, piece, HD), BF16),
        pltpu.VMEM((CHUNKS, piece, HD), BF16),
        pltpu.VMEM((8, HD), F32),
        pltpu.VMEM((MEMBERS, CHUNKS, piece, HD), BF16),
        pltpu.VMEM((MEMBERS, CHUNKS, piece, HD), BF16),
        pltpu.SemaphoreType.DMA((2, MEMBERS)),
        pltpu.SemaphoreType.DMA((2, MEMBERS)),
        pltpu.SemaphoreType.DMA((2, CHUNKS)),
        pltpu.SemaphoreType.DMA((2,)),
        pltpu.SemaphoreType.DMA((2, MEMBERS, CHUNKS)),
    ]


def head_cols(h):
    return pl.ds(pl.multiple_of(h * HD, HD), HD)


def forward_kernel(groups, q_hbm, k_hbm, v_hbm, og_hbm, gain_ref, tag_ref, mask_ref, first_ref, last_ref,
                   att_hbm, inc_ref, square_ref, cross_ref, q_ref, k_ref, v_ref, og_ref, att_ref, state_ref,
                   load_sem, store_sem, *scratch):
    tokens, width = q_ref.shape
    part = width // MEMBERS
    pairs = width // HD // 2

    def load(a, m):
        source, target = ((k_hbm, k_ref), (v_hbm, v_ref), (q_hbm, q_ref), (og_hbm, og_ref))[a]
        cols = pl.ds(m * part, part)
        return pltpu.make_async_copy(source.at[:, cols], target.at[:, cols], load_sem.at[a, m])

    def store(m):
        cols = pl.ds(m * part, part)
        return pltpu.make_async_copy(att_ref.at[:, cols], att_hbm.at[:, cols], store_sem.at[m])

    for m in range(MEMBERS):
        load(0, m).start()
        load(1, m).start()
    for a in (2, 3):
        for m in range(MEMBERS):
            load(a, m).start()

    def make_part(m):
        load(0, m).wait()
        load(1, m).wait()
        for h in range(m * part // HD, (m + 1) * part // HD):
            cols = slice(h * HD, (h + 1) * HD)
            state_ref[cols, :] = dot_tn(k_ref[:, cols] * last_ref[...], v_ref[:, cols]).astype(BF16)
        if m == MEMBERS - 1:
            for i in range(MEMBERS):
                load(2, i).wait()

    def work(low, high):
        def pair(i, carry):
            for h in (2 * i, 2 * i + 1):
                cols = head_cols(h)
                for start in range(0, tokens, ROWS):
                    stop = start + ROWS
                    rows = slice(start, stop)
                    scores = dot_nt(q_ref[rows, cols], k_ref[:stop, cols]).astype(BF16) * mask_ref[rows, :stop]
                    att_ref[rows, cols] = dot_nn(scores, v_ref[:stop, cols])
            return carry
        lax.fori_loop(low, high, pair, 0)

    exchange(groups, False, make_part, work, pairs * 3 // 8, pairs // 4, pairs, state_ref, tag_ref, inc_ref, *scratch)

    square_ref[...] = jnp.zeros_like(square_ref)
    cross_ref[...] = jnp.zeros_like(cross_ref)
    for m in range(MEMBERS):
        load(3, m).wait()

        def add(h, carry):
            cols = head_cols(h)
            inc = inc_ref[pl.ds(pl.multiple_of(h * HD, HD), HD), :]
            for start in range(0, tokens, ROWS):
                rows = slice(start, start + ROWS)
                att = att_ref[rows, cols] + dot_nn(q_ref[rows, cols] * first_ref[rows, :], inc)
                att_ref[rows, cols] = att
                square_ref[rows, :] += att * att
                cross_ref[rows, :] += gain_ref[:, cols] * og_ref[rows, cols].astype(F32) * att
            return carry
        lax.fori_loop(m * part // HD, (m + 1) * part // HD, add, 0)
        store(m).start()
    for m in range(MEMBERS):
        store(m).wait()


def delta_kernel(att_ref, og_ref, q_ref, gain_ref, inverse_ref, weight_ref, first_ref,
                 normed_ref, delta_ref, state_ref):
    for h in range(q_ref.shape[1] // HD):
        cols = slice(h * HD, (h + 1) * HD)
        att = att_ref[:, cols]
        gain = gain_ref[:, cols]
        inverse = inverse_ref[...]
        normed_ref[:, cols] = (att * inverse * gain).astype(BF16)
        delta = (inverse * (gain * og_ref[:, cols].astype(F32)) - att * weight_ref[...]).astype(BF16)
        delta_ref[:, cols] = delta
        state_ref[cols, :] = dot_tn(q_ref[:, cols] * first_ref[...], delta).astype(BF16)


def backward_kernel(groups, q_hbm, k_hbm, v_hbm, d_hbm, state_ref, tag_ref, inc_ref, mask_ref, first_ref,
                    gq_hbm, gk_hbm, gv_hbm, out_ref, q_ref, k_ref, v_ref, d_ref,
                    load_sem, store_sem, *scratch):
    tokens, width = q_ref.shape
    part = width // MEMBERS
    pairs = width // HD // 2

    def load(a, m):
        source, target = ((q_hbm, q_ref), (k_hbm, k_ref), (v_hbm, v_ref), (d_hbm, d_ref))[a]
        cols = pl.ds(m * part, part)
        return pltpu.make_async_copy(source.at[:, cols], target.at[:, cols], load_sem.at[a, m])

    def store(a):
        source, target = ((q_ref, gq_hbm), (k_ref, gk_hbm), (v_ref, gv_hbm))[a]
        return pltpu.make_async_copy(source, target, store_sem.at[a])

    for m in range(MEMBERS):
        for a in range(4):
            load(a, m).start()

    def make_part(m):
        if m == MEMBERS - 1:
            for a in range(4):
                load(a, 0).wait()

    def one(h):
        cols = head_cols(h)
        inc = inc_ref[pl.ds(pl.multiple_of(h * HD, HD), HD), :]
        grad_query = dot_nt(d_ref[:, cols] * first_ref[...], inc)
        pieces = [grad_query[r:r + ROWS] for r in range(0, tokens, ROWS)]
        for start in range(0, tokens, ROWS):
            rows = slice(start, start + ROWS)
            k, v = k_ref[rows, cols], v_ref[rows, cols]
            q, d = q_ref[start:, cols], d_ref[start:, cols]
            mask = mask_ref[rows, start:]
            scores = dot_nt(k, q).astype(BF16) * mask
            dscores = dot_nt(v, d).astype(BF16) * mask
            v_ref[rows, cols] = dot_nn(scores, d).astype(BF16)
            k_ref[rows, cols] = dot_nn(dscores, q).astype(BF16)
            more = dot_tn(dscores, k)
            for i in range(start // ROWS, tokens // ROWS):
                at = i * ROWS - start
                pieces[i] = pieces[i] + more[at:at + ROWS]
        for i, piece in enumerate(pieces):
            q_ref[i * ROWS:(i + 1) * ROWS, cols] = piece.astype(BF16)

    def work(low, high):
        def pair(i, carry):
            one(2 * i)
            one(2 * i + 1)
            return carry
        lax.fori_loop(low, high, pair, 0)
        if isinstance(low, int) and low == 0:
            for m in range(1, MEMBERS):
                for a in range(4):
                    load(a, m).wait()
        if isinstance(high, int) and high == pairs:
            for a in range(3):
                store(a).start()

    exchange(groups, True, make_part, work, pairs // MEMBERS, max(1, pairs // 8), pairs,
             state_ref, tag_ref, out_ref, *scratch)
    for a in range(3):
        store(a).wait()


def finish_kernel(k_ref, v_ref, gk_ref, gv_ref, out_ref, last_ref, grad_key_ref, grad_value_ref):
    for h in range(k_ref.shape[1] // HD):
        cols = slice(h * HD, (h + 1) * HD)
        last = last_ref[...]
        out = out_ref[cols, :]
        grad_key_ref[:, cols] = (gk_ref[:, cols].astype(F32) + dot_nt(v_ref[:, cols] * last, out)).astype(BF16)
        grad_value_ref[:, cols] = (gv_ref[:, cols].astype(F32) + dot_nn(k_ref[:, cols] * last, out)).astype(BF16)


def shards(blocks, queries, keys, values, out_grad, gain, doc_ids):
    tokens, width = queries.shape
    heads = width // HD
    width_all = HEADS * HD
    position = jnp.arange(tokens)
    same = doc_ids[:, None] == doc_ids[None, :]
    mask = (same & (position[:, None] >= position[None, :])).astype(BF16)
    mask_t = (same & (position[:, None] <= position[None, :])).astype(BF16)
    first_doc, last_doc = doc_ids[0], doc_ids[tokens - 1]
    first_rows = jnp.broadcast_to((doc_ids == first_doc).astype(BF16)[:, None], (tokens, HD))
    last_rows = jnp.broadcast_to((doc_ids == last_doc).astype(BF16)[:, None], (tokens, HD))
    tag = jnp.where(jnp.arange(8)[:, None] == 0, first_doc, last_doc).astype(F32)
    tag = jnp.broadcast_to(tag, (8, HD))
    gain = gain[None, :]

    each = 2
    wide = each * HD
    grid = (heads // each,)
    cols_spec = pl.BlockSpec((tokens, wide), lambda i: (0, i))
    gain_cols = pl.BlockSpec((1, wide), lambda i: (0, i))
    head_state = pl.BlockSpec((wide, HD), lambda i: (i, 0))
    whole = pl.BlockSpec((tokens, HD), lambda i: (0, 0))
    state_shape = jax.ShapeDtypeStruct((width, HD), BF16)
    flat_shape = jax.ShapeDtypeStruct((tokens, width), BF16)
    sums_shape = jax.ShapeDtypeStruct((tokens, HD), F32)
    params = pltpu.CompilerParams(vmem_limit_bytes=40 * 2**20)

    groups = blocks // MEMBERS
    vmem = pl.BlockSpec(memory_space=pltpu.VMEM)
    hbm = pl.BlockSpec(memory_space=pl.ANY)
    held = pltpu.VMEM((tokens, width), BF16)
    att_shape = jax.ShapeDtypeStruct((tokens, width), F32)
    attended, incoming, squares, crosses = pl.pallas_call(
        functools.partial(forward_kernel, groups),
        in_specs=[hbm] * 4 + [vmem] * 5,
        out_specs=[hbm, vmem, vmem, vmem],
        out_shape=[att_shape, state_shape, sums_shape, sums_shape],
        scratch_shapes=[held, held, held, held, pltpu.VMEM((tokens, width), F32), pltpu.VMEM((width, HD), BF16),
                        pltpu.SemaphoreType.DMA((4, MEMBERS)), pltpu.SemaphoreType.DMA((MEMBERS,))]
        + exchange_scratch(width),
        compiler_params=pltpu.CompilerParams(collective_id=0, has_side_effects=True, vmem_limit_bytes=58 * 2**20),
        name="attend",
    )(queries, keys, values, out_grad, gain, tag, mask, first_rows, last_rows)
    square_sum, cross_sum = lax.psum((jnp.sum(squares, axis=1), jnp.sum(crosses, axis=1)), "tp")
    inverse = lax.rsqrt(square_sum / width_all + NORM_EPS)
    weight = inverse**3 * cross_sum / width_all
    inverse = jnp.broadcast_to(inverse[:, None], (tokens, HD))
    weight = jnp.broadcast_to(weight[:, None], (tokens, HD))
    normed, delta, own_reverse = pl.pallas_call(
        delta_kernel, grid=grid,
        in_specs=[cols_spec, cols_spec, cols_spec, gain_cols, whole, whole, whole],
        out_specs=[cols_spec, cols_spec, head_state],
        out_shape=[flat_shape, flat_shape, state_shape],
        compiler_params=params, name="delta",
    )(attended, out_grad, queries, gain, inverse, weight, first_rows)
    grad_query, key_part, value_part, outgoing = pl.pallas_call(
        functools.partial(backward_kernel, groups),
        in_specs=[hbm] * 4 + [vmem] * 5,
        out_specs=[hbm, hbm, hbm, vmem],
        out_shape=[flat_shape, flat_shape, flat_shape, state_shape],
        scratch_shapes=[held, held, held, held,
                        pltpu.SemaphoreType.DMA((4, MEMBERS)), pltpu.SemaphoreType.DMA((3,))]
        + exchange_scratch(width),
        compiler_params=pltpu.CompilerParams(collective_id=1, has_side_effects=True, vmem_limit_bytes=58 * 2**20),
        name="grads",
    )(queries, keys, values, delta, own_reverse, tag, incoming, mask_t, first_rows)
    grad_key, grad_value = pl.pallas_call(
        finish_kernel, grid=grid,
        in_specs=[cols_spec] * 4 + [head_state, whole],
        out_specs=[cols_spec] * 2, out_shape=[flat_shape] * 2,
        compiler_params=params, name="finish",
    )(keys, values, key_part, value_part, outgoing, last_rows)
    return normed, grad_query, grad_key, grad_value


def solution(mesh):
    in_specs = (P("ctx", "tp"), P("ctx", "tp"), P("ctx", "tp"), P("ctx", "tp"), P("tp"), P("ctx"))
    out_specs = (P("ctx", "tp"), P("ctx", "tp"), P("ctx", "tp"), P("ctx", "tp"))
    return jax.shard_map(functools.partial(shards, mesh.shape["ctx"]), mesh=mesh, in_specs=in_specs,
                         out_specs=out_specs, check_vma=False)
```
